1024 devices in a mesh: node: 64 (over y, z), xnode: 16 (over x, core).
Axes of the slice: x: 8, y: 8, z: 8, core: 2. Of those that a mesh axis runs over, the one named last changes fastest.
Arguments:
- pooled: bfloat16 [3072, 65536], P('xnode', 'node'), may hold values from -6 to 6
- counts: int32 [3072, 256], P('xnode', 'node'), may hold values from 0 to 12, as said below
- dims: int32 [256], P('node'), may hold values from 128 to 512, as said below
- proj: bfloat16 [65536, 128], P('node'), may hold values from -0.375 to 0.375
- v_weight: bfloat16 [3, 32768, 256], P(None, 'node'), may hold values from -0.03125 to 0.03125
- u_weight: bfloat16 [3, 256, 32768], P(None, None, 'node'), may hold values from -0.375 to 0.375
- bias: float32 [3, 32768], P(None, 'node'), may hold values from -3 to 3
- cotangent: bfloat16 [3072, 32768], P('xnode', 'node'), may hold values from -6 to 6
Outputs:
- row_grads: bfloat16 [65536, 3072], P(('node', 'xnode'))
- proj_grad: float32 [65536, 128], P(('node', 'xnode'))
The draws below stay inside these ranges and needn't reach their ends.
Inputs may be any that keep to these rules, and one draw needn't show every extreme that they name: counts of every feature have a largest value of their own between 4 and 12, reached in the first sample. `dims`: the widths of each aligned block of 4 features sum to 1024; each is 128, 256 or 512.
All inputs are finite; a program needn't handle non-finite values.
Results may differ from the reference program's by a relative error of at most 0.025.
Values may be sent and summed in bfloat16 or wider, within the bound.
A program may use at most 32 MiB of HBM per device.

```python
import jax
import jax.numpy as jnp
from jax import lax

FEAT_DEV = 4
E = 128
R = 256
LAYERS = 3
DPACK = 1024
CMAX = 12
B_GRP = 192
F = 256
FW = 32768
TOKENS = 3072
N_NODE = 64
N_XNODE = 16


def draw_counts(key, part):
    key = jax.random.fold_in(key, 11)
    first_key, second_key = jax.random.split(key)
    largest = jax.random.randint(first_key, (F,), CMAX // 3, CMAX + 1)
    largest = largest.at[0].set(CMAX)
    raw_draw = jax.random.randint(second_key, (TOKENS, F), 0, 1 << 20)
    values = raw_draw % (largest[None, :] + 1)
    values = values.at[0, :].set(largest)
    return values.astype(jnp.int32)


def draw_dims(key, part):
    key = jax.random.fold_in(key, 23)
    first_key, second_key = jax.random.split(key)
    nblock = F // FEAT_DEV
    uneven = jax.random.randint(first_key, (nblock, 1), 0, 2)
    uneven = uneven.at[0, 0].set(1)
    pattern = jnp.array([DPACK // 2, DPACK // 4, DPACK // 8, DPACK // 8], jnp.int32)
    scores = jax.random.randint(second_key, (nblock, FEAT_DEV), 0, 1 << 20) * FEAT_DEV
    scores = scores + jnp.arange(FEAT_DEV, dtype=jnp.int32)[None, :]
    order = jnp.argsort(scores, axis=1)
    shuffled = pattern[order]
    result = jnp.where(uneven == 1, shuffled, DPACK // 4)
    return result.reshape(F).astype(jnp.int32)


def shard_levels(rng, shape, shards, smallest, high):
    gain, own = 1.0, jax.random.fold_in(rng, 6)
    for position, parts in shards:
        steps = jnp.exp(jax.random.uniform(jax.random.fold_in(own, position), (parts,), jnp.float32, smallest / len(shards), high / len(shards)))
        gain = gain * jnp.repeat(steps, shape[position] // parts).reshape([-1 if axis == position else 1 for axis in range(len(shape))])
    return gain


def gaussian(own_key, shape, deviation, most, shards=(), kind=jnp.bfloat16):
    entries = jax.random.normal(own_key, shape, jnp.float32) * deviation
    if len(shards) > 0:
        entries = shard_levels(own_key, shape, shards, -0.22, 0.18) * entries
    return jnp.clip(entries, min=-most, max=most).astype(kind)


def setup_inputs(seed: int = 0) -> dict:
    splits = jax.random.split(jax.random.key(seed), 9)
    pooled = gaussian(splits[0], (TOKENS, N_NODE * DPACK), 1.0, 6.0, ((0, 16), (1, 64)))
    counts = draw_counts(jax.random.fold_in(splits[8], 71), 0)
    dims = draw_dims(jax.random.fold_in(splits[8], 71), 0)
    proj = gaussian(splits[3], (N_NODE * DPACK, E), (DPACK // 4) ** -0.5, 0.375, ((0, 64),))
    v_weight = gaussian(splits[4], (LAYERS, FW, R), FW ** -0.5, 0.03125, ((1, 64),))
    u_weight = gaussian(splits[5], (LAYERS, R, FW), R ** -0.5, 0.375, ((2, 64),))
    bias = gaussian(splits[6], (LAYERS, FW), 0.5, 3.0, ((1, 64),), jnp.float32)
    cotangent = gaussian(splits[7], (TOKENS, FW), 1.0, 6.0, ((0, 16), (1, 64)))
    return dict(pooled=pooled, counts=counts, dims=dims, proj=proj, v_weight=v_weight, u_weight=u_weight, bias=bias, cotangent=cotangent)


def segment_table(dims):
    blocks = dims.reshape(-1, FEAT_DEV)
    ends = jnp.cumsum(blocks, axis=1).astype(jnp.int32)
    starts = (ends - blocks).astype(jnp.int32)
    column = jnp.arange(DPACK, dtype=jnp.int32)
    inside = (column >= starts[..., None]) & (column < ends[..., None])
    return inside.astype(jnp.float32)


def reference(pooled, counts, dims, proj, v_weight, u_weight, bias, cotangent):
    one_hot = segment_table(dims)
    nblock = one_hot.shape[0]
    proj_blocks = proj.reshape(nblock, DPACK, E).astype(jnp.float32)
    widened = jnp.einsum('njd,nde->ndje', one_hot, proj_blocks).reshape(nblock, DPACK, FEAT_DEV * E)

    def group_backward(inputs):
        pool_grp, count_grp, cot_grp = inputs
        live = (count_grp > 0).astype(jnp.float32).reshape(B_GRP, nblock, FEAT_DEV)
        mask_wide = jnp.einsum('bnj,njd->bnd', live, one_hot)
        masked = (pool_grp.reshape(B_GRP, nblock, DPACK).astype(jnp.float32) * mask_wide).astype(jnp.bfloat16)
        start = jnp.einsum('bnd,nde->bne', masked.astype(jnp.float32), widened)
        start = start.reshape(B_GRP, FW).astype(jnp.bfloat16)
        base = start.astype(jnp.float32)
        state = base
        outputs = []
        for layer in range(LAYERS):
            operand = state.astype(jnp.bfloat16)
            lowrank = jnp.dot(operand, v_weight[layer], preferred_element_type=jnp.float32).astype(jnp.bfloat16)
            upward = jnp.dot(lowrank, u_weight[layer], preferred_element_type=jnp.float32) + bias[layer]
            outputs.append(upward)
            state = base * upward + state
        grad = cot_grp.astype(jnp.float32)
        accum = jnp.zeros((B_GRP, FW), jnp.float32)
        for layer in range(LAYERS - 1, -1, -1):
            accum = accum + grad * outputs[layer]
            dupward = (grad * base).astype(jnp.bfloat16)
            dlow = jnp.dot(dupward, u_weight[layer].T, preferred_element_type=jnp.float32).astype(jnp.bfloat16)
            grad = grad + jnp.dot(dlow, v_weight[layer].T, preferred_element_type=jnp.float32)
        dstart = (accum + grad).astype(jnp.bfloat16)
        dstart_blocks = dstart.reshape(B_GRP, nblock, FEAT_DEV * E).astype(jnp.float32)
        dpool = jnp.einsum('bne,nde->bnd', dstart_blocks, widened)
        scale = live / jnp.maximum(count_grp.astype(jnp.float32).reshape(B_GRP, nblock, FEAT_DEV), 1.0)
        scale_wide = jnp.einsum('bnj,njd->bnd', scale, one_hot)
        row_part = (dpool * scale_wide).astype(jnp.bfloat16).reshape(B_GRP, nblock * DPACK)
        full_term = jnp.einsum('bnd,bne->nde', masked.astype(jnp.float32), dstart_blocks)
        full_term = full_term.reshape(nblock, DPACK, FEAT_DEV, E)
        chosen = jnp.sum(full_term * jnp.transpose(one_hot, (0, 2, 1))[..., None], axis=2)
        return row_part, chosen

    pool_groups = pooled.reshape(N_XNODE, B_GRP, N_NODE * DPACK)
    count_groups = counts.reshape(N_XNODE, B_GRP, F)
    cot_groups = cotangent.reshape(N_XNODE, B_GRP, FW)
    row_parts, proj_parts = lax.map(group_backward, (pool_groups, count_groups, cot_groups))
    row_grads = row_parts.reshape(TOKENS, N_NODE * DPACK).T
    proj_grad = jnp.sum(proj_parts, axis=0).reshape(N_NODE * DPACK, E)
    return row_grads, proj_grad
```

```python
import functools

import jax
import jax.numpy as jnp
from jax import lax
from jax.experimental import pallas as pl
from jax.experimental.pallas import tpu as pltpu
from jax.sharding import PartitionSpec as P

LAYERS = 3
SIDE = 8
CORES = 2
GROUPS = SIDE * CORES
SAMPLES = 192
RANK = 256
WIDTH = 512
FEATS = 4
E = 128
PACKED = 1024
PIECE = PACKED // GROUPS
SHARD = 48
F32 = jnp.float32
BF16 = jnp.bfloat16

NN = (((1,), (0,)), ((), ()))
NT = (((1,), (1,)), ((), ()))
TN = (((0,), (0,)), ((), ()))


def dot(a, b, dims=NN):
    return lax.dot_general(a, b, dims, preferred_element_type=F32)


def kernel(
    dims_ref, counts_ref, pooled_ref, proj_ref, v_ref, u_ref, bias_ref, cot_ref,
    row_ref, pg_ref,
    base, state, grads, ups, scale,
    send1, recv1, sum1, recv2, gath,
    wsend, wrecv, dsend, drecv, pgall,
    s1_sem, r1_sem, s2_sem, r2_sem, s3_sem, r3_sem,
    ws_sem, wr_sem, ds_sem, dr_sem, fs_sem, fr_sem,
):
    node = lax.axis_index("node")
    group = lax.axis_index("xnode")
    y, z = node // SIDE, node % SIDE
    x, core = group // CORES, group % CORES
    here = (y, z)

    def along(axis, to):
        return (to * SIDE + z, group) if axis == 0 else (y * SIDE + to, group)

    def copy(src, dst, ssem, rsem, device):
        return pltpu.make_async_remote_copy(
            src_ref=src, dst_ref=dst, send_sem=ssem, recv_sem=rsem,
            device_id=device, device_id_type=pl.DeviceIdType.MESH,
        )

    barrier = pltpu.get_barrier_semaphore()

    def greet(d, c):
        for axis in (0, 1):
            to = lax.rem(here[axis] + d, SIDE)
            pl.semaphore_signal(
                barrier, inc=1, device_id=along(axis, to), device_id_type=pl.DeviceIdType.MESH
            )
        return c

    def greet_x(d, c):
        to = lax.rem(group + d, GROUPS)
        pl.semaphore_signal(
            barrier, inc=1, device_id=(node, to), device_id_type=pl.DeviceIdType.MESH
        )
        return c

    lax.fori_loop(1, SIDE, greet, 0)
    lax.fori_loop(1, GROUPS, greet_x, 0)

    ends = []
    total = jnp.int32(0)
    for j in range(FEATS):
        total = total + dims_ref[j]
        ends.append(total)
    starts = [jnp.int32(0)] + ends[:-1]
    rows = lax.broadcasted_iota(jnp.int32, (PACKED, E), 0)
    proj32 = proj_ref[...].astype(F32)
    widened = jnp.concatenate(
        [
            jnp.where((rows >= starts[j]) & (rows < ends[j]), proj32, 0.0).astype(BF16)
            for j in range(FEATS)
        ],
        axis=1,
    )
    counts = counts_ref[...].astype(F32)
    wide = [jnp.broadcast_to(counts[:, j : j + 1], (SAMPLES, E)) for j in range(FEATS)]
    live = jnp.concatenate([jnp.where(w > 0, 1.0, 0.0) for w in wide], axis=1)
    scale[...] = live / jnp.concatenate([jnp.maximum(w, 1.0) for w in wide], axis=1)
    start = dot(pooled_ref[...], widened) * live
    base[...] = start.astype(BF16)
    state[...] = base[...].astype(F32)

    def pick(c, parts):
        out = parts[0]
        for j in range(1, FEATS):
            inside = jnp.full(parts[0].shape, c * E, jnp.int32) >= starts[j]
            out = jnp.where(inside, parts[j], out)
        return out

    pl.semaphore_wait(barrier, 2 * (SIDE - 1) + GROUPS - 1)

    def start1(r, k, partial):
        rounded = partial.astype(BF16)
        for i in range(SIDE):
            a, b = i % 4, i // 4
            send1[r, k, i] = rounded[a * SHARD : (a + 1) * SHARD, b * E : (b + 1) * E]

        def one(d, c):
            to = lax.rem(here[k] + d, SIDE)
            copy(
                send1.at[r, k, to], recv1.at[r, k, d - 1], s1_sem.at[r, k], r1_sem.at[r, k],
                along(k, to),
            ).start()
            return c

        lax.fori_loop(1, SIDE, one, 0)

    def settle(ref, sem):
        pltpu.make_async_copy(ref, ref, sem).wait()

    def start2(r, k):
        settle(recv1.at[r, k], r1_sem.at[r, k])
        acc = send1[r, k, here[k]].astype(F32)
        for d in range(SIDE - 1):
            acc = acc + recv1[r, k, d].astype(F32)
        sum1[r, k] = acc.astype(BF16)

        def one(d, c):
            to = lax.rem(here[1 - k] + d, SIDE)
            copy(
                sum1.at[r, k], recv2.at[r, k, d - 1], s2_sem.at[r, k], r2_sem.at[r, k],
                along(1 - k, to),
            ).start()
            return c

        lax.fori_loop(1, SIDE, one, 0)

    def start3(r, k):
        settle(recv2.at[r, k], r2_sem.at[r, k])
        acc = sum1[r, k].astype(F32)
        for d in range(SIDE - 1):
            acc = acc + recv2[r, k, d].astype(F32)
        gath[r, k, here[k]] = acc.astype(BF16)

        def one(d, c):
            to = lax.rem(here[k] + d, SIDE)
            mine = gath.at[r, k, here[k]]
            copy(mine, mine, s3_sem.at[r, k], r3_sem.at[r, k], along(k, to)).start()
            return c

        lax.fori_loop(1, SIDE, one, 0)

    def finish(r, k):
        settle(recv1.at[r, k], r3_sem.at[r, k])
        whole = gath[r, k]
        return jnp.concatenate(
            [whole[0:4].reshape(SAMPLES, E), whole[4:8].reshape(SAMPLES, E)], axis=1
        )

    def start_forward(r):
        start1(r, 0, dot(state[...].astype(BF16), v_ref[r]))

    def start_backward(r):
        product = (grads[r] * base[...].astype(F32)).astype(BF16)
        start1(r, 1, dot(product, u_ref[LAYERS - 1 - r], NT))

    start_forward(0)
    grads[0] = cot_ref[...].astype(F32)
    start_backward(0)

    for c in range(SIDE):
        cols = pooled_ref[:, c * E : (c + 1) * E].astype(F32)
        wsend[c] = (cols * pick(c, wide)).astype(BF16)

    def send_w(d, c):
        to = lax.rem(group + d, GROUPS)
        copy(wsend.at[to // CORES], wrecv.at[group], ws_sem, wr_sem, (node, to)).start()
        return c

    lax.fori_loop(1, GROUPS, send_w, 0)
    wrecv[group] = wsend[x]

    for r in range(LAYERS):
        start2(r, 0)
        start2(r, 1)
        start3(r, 0)
        start3(r, 1)
        up = dot(finish(r, 0), u_ref[r]) + bias_ref[r : r + 1, :]
        ups[r] = up
        if r < LAYERS - 1:
            state[...] = base[...].astype(F32) * up + state[...]
            start_forward(r + 1)
        grads[r + 1] = grads[r] + dot(finish(r, 1), v_ref[LAYERS - 1 - r], NT)
        if r < LAYERS - 1:
            start_backward(r + 1)

    acc = grads[0] * ups[2] + grads[1] * ups[1] + grads[2] * ups[0] + grads[3]
    scaled = acc * scale[...]
    parts = [scaled[:, j * E : (j + 1) * E] for j in range(FEATS)]
    for c in range(SIDE):
        dsend[c] = pick(c, parts).astype(BF16)

    def send_d(d, c):
        to = lax.rem(x + d, SIDE)
        copy(
            dsend.at[to], drecv.at[group], ds_sem, dr_sem.at[d - 1], (node, to * CORES + core)
        ).start()
        return c

    lax.fori_loop(1, SIDE, send_d, 0)
    sibling = (node, x * CORES + 1 - core)
    drecv[group] = dsend[x]
    copy(dsend.at[x], drecv.at[group], fs_sem, fr_sem, sibling).start()

    def forward_d(d, c):
        origin = lax.rem(x + SIDE - d, SIDE) * CORES + core
        block = drecv.at[origin]
        settle(block, dr_sem.at[d - 1])
        copy(block, block, fs_sem, fr_sem, sibling).start()
        return c

    lax.fori_loop(1, SIDE, forward_d, 0)
    settle(wrecv.at[0 : GROUPS - 1], wr_sem)
    settle(drecv.at[0:SIDE], fr_sem)
    every = drecv[...].reshape(GROUPS * SAMPLES, E)
    mine = proj_ref[pl.ds(pl.multiple_of(group * PIECE, PIECE), PIECE), :]
    row_ref[...] = dot(mine, every, NT).astype(BF16)
    pgall[...] = dot(wrecv[...].reshape(GROUPS * SAMPLES, E), every, TN)
    pg_ref[...] = pgall[pl.ds(pl.multiple_of(core * PIECE, PIECE), PIECE), :]

    for r in range(LAYERS):
        for k in range(2):
            settle(recv1.at[r, k], s1_sem.at[r, k])
            settle(recv1.at[r, k], s2_sem.at[r, k])
            settle(recv1.at[r, k], s3_sem.at[r, k])
    settle(wrecv.at[0 : GROUPS - 1], ws_sem)
    settle(drecv.at[0 : SIDE - 1], ds_sem)
    settle(drecv.at[0:SIDE], fs_sem)


def on_device(pooled, counts, dims, proj, v_weight, u_weight, bias, cotangent):
    vmem = pl.BlockSpec(memory_space=pltpu.VMEM)
    smem = pl.BlockSpec(memory_space=pltpu.SMEM)
    dma = pltpu.SemaphoreType.DMA
    pair = (LAYERS, 2)
    return pl.pallas_call(
        kernel,
        out_shape=(
            jax.ShapeDtypeStruct((PIECE, GROUPS * SAMPLES), BF16),
            jax.ShapeDtypeStruct((PIECE, E), F32),
        ),
        in_specs=[smem] + [vmem] * 7,
        out_specs=(vmem, vmem),
        scratch_shapes=[
            pltpu.VMEM((SAMPLES, WIDTH), BF16),
            pltpu.VMEM((SAMPLES, WIDTH), F32),
            pltpu.VMEM((LAYERS + 1, SAMPLES, WIDTH), F32),
            pltpu.VMEM((LAYERS, SAMPLES, WIDTH), F32),
            pltpu.VMEM((SAMPLES, WIDTH), F32),
            pltpu.VMEM(pair + (SIDE, SHARD, E), BF16),
            pltpu.VMEM(pair + (SIDE - 1, SHARD, E), BF16),
            pltpu.VMEM(pair + (SHARD, E), BF16),
            pltpu.VMEM(pair + (SIDE - 1, SHARD, E), BF16),
            pltpu.VMEM(pair + (SIDE, SHARD, E), BF16),
            pltpu.VMEM((SIDE, SAMPLES, E), BF16),
            pltpu.VMEM((GROUPS, SAMPLES, E), BF16),
            pltpu.VMEM((SIDE, SAMPLES, E), BF16),
            pltpu.VMEM((GROUPS, SAMPLES, E), BF16),
            pltpu.VMEM((E, E), F32),
            dma(pair), dma(pair), dma(pair), dma(pair), dma(pair), dma(pair),
            dma, dma, dma, dma((SIDE - 1,)), dma, dma,
        ],
        compiler_params=pltpu.CompilerParams(
            collective_id=0, has_side_effects=True, vmem_limit_bytes=40 * 1024 * 1024
        ),
        cost_estimate=pl.CostEstimate(
            flops=1_500_000_000, bytes_accessed=3_000_000, transcendentals=0
        ),
    )(dims, counts, pooled, proj, v_weight, u_weight, bias, cotangent)


def solution(mesh):
    in_specs = (
        P("xnode", "node"),
        P("xnode", "node"),
        P("node"),
        P("node", None),
        P(None, "node", None),
        P(None, None, "node"),
        P(None, "node"),
        P("xnode", "node"),
    )
    out_specs = (P(("node", "xnode"), None), P(("node", "xnode"), None))
    return jax.shard_map(
        on_device, mesh=mesh, in_specs=in_specs, out_specs=out_specs, check_vma=False
    )
```

```python
import functools

import jax
import jax.numpy as jnp
from jax import lax
from jax.experimental import pallas as pl
from jax.experimental.pallas import tpu as pltpu
from jax.sharding import PartitionSpec as P

LAYERS = 3
SIDE = 8
CORES = 2
GROUPS = SIDE * CORES
SAMPLES = 192
RANK = 256
WIDTH = 512
FEATS = 4
E = 128
PACKED = 1024
PIECE = PACKED // GROUPS
SHARD = 48
ORDER = (4, 3, 5, 2, 6, 1, 7)
F32 = jnp.float32
BF16 = jnp.bfloat16

NN = (((1,), (0,)), ((), ()))
NT = (((1,), (1,)), ((), ()))
TN = (((0,), (0,)), ((), ()))


def dot(a, b, dims=NN):
    return lax.dot_general(a, b, dims, preferred_element_type=F32)


def kernel(
    dims_hbm, counts_hbm, pooled_hbm, proj_hbm, v_hbm, u_hbm, bias_hbm, cot_hbm,
    row_ref, pg_ref,
    dims_ref, counts_ref, pooled_ref, proj_ref, v_ref, u_ref, bias_ref, cot_ref,
    base, state, grads, ups, scale, cots, pre,
    send1, recv1, sum1, recv2, gath,
    wsend, wrecv, wturn, dsend, drecv, pgown, pgin,
    in_sem, s1_sem, r1_sem, s2_sem, r2_sem, s3_sem, r3_sem,
    ws_sem, wr_sem, ds_sem, dr_sem, fs_sem, fr_sem, ps_sem, pr_sem,
):
    node = lax.axis_index("node")
    group = lax.axis_index("xnode")
    y, z = node // SIDE, node % SIDE
    x, core = group // CORES, group % CORES
    here = (y, z)

    def along(axis, to):
        return (to * SIDE + z, group) if axis == 0 else (y * SIDE + to, group)

    def copy(src, dst, ssem, rsem, device):
        return pltpu.make_async_remote_copy(
            src_ref=src, dst_ref=dst, send_sem=ssem, recv_sem=rsem,
            device_id=device, device_id_type=pl.DeviceIdType.MESH,
        )

    barrier = pltpu.get_barrier_semaphore()
    for d in ORDER:
        for axis in (0, 1):
            to = lax.rem(here[axis] + d, SIDE)
            pl.semaphore_signal(
                barrier, inc=1, device_id=along(axis, to), device_id_type=pl.DeviceIdType.MESH
            )

    def greet_x(d, c):
        to = lax.rem(group + d, GROUPS)
        pl.semaphore_signal(
            barrier, inc=1, device_id=(node, to), device_id_type=pl.DeviceIdType.MESH
        )
        return c

    lax.fori_loop(1, GROUPS, greet_x, 0)

    pairs = {
        "dims": (dims_hbm, dims_ref),
        "counts": (counts_hbm, counts_ref),
        "pooled": (pooled_hbm, pooled_ref),
        "proj": (proj_hbm, proj_ref),
        "v0": (v_hbm.at[0], v_ref.at[0]),
        "u2": (u_hbm.at[2], u_ref.at[2]),
        "cot": (cot_hbm, cot_ref),
        "u0": (u_hbm.at[0], u_ref.at[0]),
        "v2": (v_hbm.at[2], v_ref.at[2]),
        "bias": (bias_hbm, bias_ref),
        "v1": (v_hbm.at[1], v_ref.at[1]),
        "u1": (u_hbm.at[1], u_ref.at[1]),
    }
    loads = {
        name: pltpu.make_async_copy(src, dst, in_sem.at[i])
        for i, (name, (src, dst)) in enumerate(pairs.items())
    }
    for load in loads.values():
        load.start()

    loads["dims"].wait()
    ends = []
    total = jnp.int32(0)
    for j in range(FEATS):
        total = total + dims_ref[j]
        ends.append(total)
    starts = [jnp.int32(0)] + ends[:-1]

    def inside(c, j):
        spot = jnp.full((SAMPLES, E), c * E, jnp.int32)
        return (spot >= starts[j]) & (spot < ends[j])

    def pick(c, parts):
        spot = jnp.full((SAMPLES, E), c * E, jnp.int32)
        out = parts[0]
        for j in range(1, FEATS):
            out = jnp.where(spot >= starts[j], parts[j], out)
        return out

    loads["counts"].wait()
    counts = counts_ref[...].astype(F32).astype(BF16)
    lane = lax.broadcasted_iota(jnp.int32, (FEATS, WIDTH), 1)
    first = lax.broadcasted_iota(jnp.int32, (FEATS, WIDTH), 0) * E
    spread = jnp.where((lane >= first) & (lane < first + E), 1.0, 0.0).astype(BF16)
    scale[...] = dot(counts, spread, TN)
    loads["pooled"].wait()
    loads["proj"].wait()
    blocks = [
        dot(pooled_ref[:, c * E : (c + 1) * E], proj_ref[c * E : (c + 1) * E, :])
        for c in range(SIDE)
    ]
    for j in range(FEATS):
        own = slice(j * E, (j + 1) * E)
        start = jnp.zeros((SAMPLES, E), F32)
        for c in range(SIDE):
            start = start + jnp.where(inside(c, j), blocks[c], 0.0)
        start = jnp.where(scale[:, own] > 0, start, 0.0).astype(BF16)
        base[:, own] = start
        state[:, own] = start.astype(F32)

    def start1(r, k, partial):
        rounded = partial.astype(BF16)
        for i in range(SIDE):
            a, b = i % 4, i // 4
            send1[r, k, i] = rounded[a * SHARD : (a + 1) * SHARD, b * E : (b + 1) * E]
        if r == 0 and k == 0:
            pl.semaphore_wait(barrier, 2 * (SIDE - 1) + GROUPS - 1)
        for d in ORDER:
            to = lax.rem(here[k] + d, SIDE)
            copy(
                send1.at[r, k, to], recv1.at[r, k, d - 1], s1_sem.at[r, k], r1_sem.at[r, k],
                along(k, to),
            ).start()

    def settle(ref, sem):
        pltpu.make_async_copy(ref, ref, sem).wait()

    def start2(r, k):
        settle(recv1.at[r, k], r1_sem.at[r, k])
        acc = send1[r, k, here[k]].astype(F32)
        for d in range(SIDE - 1):
            acc = acc + recv1[r, k, d].astype(F32)
        sum1[r, k] = acc.astype(BF16)
        for d in ORDER:
            to = lax.rem(here[1 - k] + d, SIDE)
            copy(
                sum1.at[r, k], recv2.at[r, k, d - 1], s2_sem.at[r, k], r2_sem.at[r, k],
                along(1 - k, to),
            ).start()

    def start3(r, k):
        settle(recv2.at[r, k], r2_sem.at[r, k])
        acc = sum1[r, k].astype(F32)
        for d in range(SIDE - 1):
            acc = acc + recv2[r, k, d].astype(F32)
        mine = gath.at[r, k, here[k]]
        gath[r, k, here[k]] = acc.astype(BF16)
        for d in ORDER:
            to = lax.rem(here[k] + d, SIDE)
            copy(mine, mine, s3_sem.at[r, k], r3_sem.at[r, k], along(k, to)).start()

    def finish(r, k):
        settle(recv1.at[r, k], r3_sem.at[r, k])
        whole = gath[r, k]
        return jnp.concatenate(
            [whole[0:4].reshape(SAMPLES, E), whole[4:8].reshape(SAMPLES, E)], axis=1
        )

    def start_forward(r):
        start1(r, 0, dot(state[...].astype(BF16), v_ref[r]))

    def start_backward(r):
        product = (grads[r] * base[...].astype(F32)).astype(BF16)
        start1(r, 1, dot(product, u_ref[LAYERS - 1 - r], NT))

    def share_w():
        column = lax.broadcasted_iota(jnp.int32, (FEATS, PACKED), 1)
        row = lax.broadcasted_iota(jnp.int32, (FEATS, PACKED), 0)
        low = jnp.zeros((FEATS, PACKED), jnp.int32)
        high = low
        for j in range(FEATS):
            low = jnp.where(row == j, starts[j], low)
            high = jnp.where(row == j, ends[j], high)
        member = jnp.where((column >= low) & (column < high), 1.0, 0.0).astype(BF16)
        weight = dot(counts, member, TN)
        for c in range(SIDE):
            own = slice(c * E, (c + 1) * E)
            wsend[c] = (pooled_ref[:, own].astype(F32) * weight[:, own]).astype(BF16)
        for d in ORDER:
            to = lax.rem(x + d, SIDE)
            copy(
                wsend.at[to], wrecv.at[x], ws_sem, wr_sem, (node, to * CORES + core)
            ).start()
        wrecv[x] = wsend[x]

    loads["v0"].wait()
    start_forward(0)
    loads["cot"].wait()
    grads[0] = cot_ref[...].astype(F32)
    loads["u2"].wait()
    start_backward(0)

    wide = scale[...]
    scale[...] = jnp.where(wide > 0, 1.0, 0.0) / jnp.maximum(wide, 1.0)
    for name in ("u0", "v2", "bias", "v1", "u1"):
        loads[name].wait()

    for r in range(LAYERS):
        last = r == LAYERS - 1
        start2(r, 0)
        start2(r, 1)
        if r == 0:
            share_w()
        start3(r, 0)
        start3(r, 1)
        if r == 1:
            settle(wrecv.at[0 : SIDE - 1], wr_sem)
            for c in range(SIDE):
                wturn[c] = wrecv[c].T
        if last:
            cot = grads[0]
            pre[...] = scale[...] * (
                grads[1] * ups[1] + grads[2] * ups[0] + grads[2] + cot * bias_ref[2:3, :]
            )
            cots[...] = scale[...] * cot
        up = dot(finish(r, 0), u_ref[r])
        if last:
            pre[...] = pre[...] + cots[...] * up
        else:
            up = up + bias_ref[r : r + 1, :]
            ups[r] = up
            state[...] = base[...].astype(F32) * up + state[...]
            start_forward(r + 1)
        down = dot(finish(r, 1), v_ref[LAYERS - 1 - r], NT)
        if last:
            pre[...] = pre[...] + scale[...] * down
        else:
            grads[r + 1] = grads[r] + down
            start_backward(r + 1)

    parts = [pre[:, j * E : (j + 1) * E] for j in range(FEATS)]
    for c in range(SIDE):
        dsend[c] = pick(c, parts).astype(BF16)
    for d in ORDER:
        to = lax.rem(x + d, SIDE)
        copy(
            dsend.at[to], drecv.at[group], ds_sem, dr_sem.at[d], (node, to * CORES + core)
        ).start()
    sibling = (node, x * CORES + 1 - core)
    copy(dsend.at[x], drecv.at[group], fs_sem, fr_sem.at[0], sibling).start()
    drecv[group] = dsend[x]

    for r in range(LAYERS):
        for k in range(2):
            settle(recv1.at[r, k], s1_sem.at[r, k])
            settle(recv1.at[r, k], s2_sem.at[r, k])
            settle(recv1.at[r, k], s3_sem.at[r, k])
    settle(wrecv.at[0 : SIDE - 1], ws_sem)

    mine = proj_ref[pl.ds(pl.multiple_of(group * PIECE, PIECE), PIECE), :]
    half = pl.ds(pl.multiple_of(core * PIECE, PIECE), PIECE)
    other = pl.ds(pl.multiple_of((1 - core) * PIECE, PIECE), PIECE)

    def use(d):
        chip = lax.rem(x + SIDE - d, SIDE)
        settle(drecv.at[chip * CORES + 1 - core], fr_sem.at[d])
        pair = drecv[pl.ds(chip * CORES, CORES)].reshape(CORES * SAMPLES, E)
        at = pl.ds(pl.multiple_of(chip * (CORES * SAMPLES), CORES * SAMPLES), CORES * SAMPLES)
        row_ref[:, at] = dot(mine, pair, NT).astype(BF16)

    pgown[...] = dot(wturn[x], dsend[x])
    waiting = [0]
    for d in ORDER:
        chip = lax.rem(x + SIDE - d, SIDE)
        block = drecv.at[chip * CORES + core]
        settle(block, dr_sem.at[d])
        copy(block, block, fs_sem, fr_sem.at[d], sibling).start()
        pgown[...] = pgown[...] + dot(wturn[chip], block[...])
        waiting.append(d)
        if d == ORDER[-1]:
            parting = copy(pgown.at[other], pgin, ps_sem, pr_sem, sibling)
            parting.start()
        if len(waiting) > 2:
            use(waiting.pop(0))
    for d in waiting:
        use(d)
    parting.wait()
    pg_ref[...] = pgown[half, :] + pgin[...]
    settle(drecv.at[0 : SIDE - 1], ds_sem)
    settle(drecv.at[0:SIDE], fs_sem)


def store_kernel(row_ref, pg_ref, row_out, pg_out, sems):
    moves = [
        pltpu.make_async_copy(row_ref, row_out, sems.at[0]),
        pltpu.make_async_copy(pg_ref, pg_out, sems.at[1]),
    ]
    for move in moves:
        move.start()
    for move in moves:
        move.wait()


def store(row_grads, proj_grad):
    vmem = pl.BlockSpec(memory_space=pltpu.VMEM)
    hbm = pl.BlockSpec(memory_space=pl.ANY)
    return pl.pallas_call(
        store_kernel,
        out_shape=(
            pltpu.HBM(row_grads.shape, row_grads.dtype),
            pltpu.HBM(proj_grad.shape, proj_grad.dtype),
        ),
        in_specs=[vmem, vmem],
        out_specs=(hbm, hbm),
        scratch_shapes=[pltpu.SemaphoreType.DMA((2,))],
    )(row_grads, proj_grad)


def on_device(pooled, counts, dims, proj, v_weight, u_weight, bias, cotangent):
    vmem = pl.BlockSpec(memory_space=pltpu.VMEM)
    hbm = pl.BlockSpec(memory_space=pl.ANY)
    dma = pltpu.SemaphoreType.DMA
    pair = (LAYERS, 2)
    inputs = (dims, counts.T, pooled, proj, v_weight, u_weight, bias, cotangent)
    results = pl.pallas_call(
        kernel,
        out_shape=(
            jax.ShapeDtypeStruct((PIECE, GROUPS * SAMPLES), BF16),
            jax.ShapeDtypeStruct((PIECE, E), F32),
        ),
        in_specs=[hbm] * 8,
        out_specs=(vmem, vmem),
        scratch_shapes=[pltpu.SMEM(dims.shape, dims.dtype)]
        + [pltpu.VMEM(a.shape, a.dtype) for a in inputs[1:]]
        + [
            pltpu.VMEM((SAMPLES, WIDTH), BF16),
            pltpu.VMEM((SAMPLES, WIDTH), F32),
            pltpu.VMEM((LAYERS, SAMPLES, WIDTH), F32),
            pltpu.VMEM((LAYERS - 1, SAMPLES, WIDTH), F32),
            pltpu.VMEM((SAMPLES, WIDTH), F32),
            pltpu.VMEM((SAMPLES, WIDTH), F32),
            pltpu.VMEM((SAMPLES, WIDTH), F32),
            pltpu.VMEM(pair + (SIDE, SHARD, E), BF16),
            pltpu.VMEM(pair + (SIDE - 1, SHARD, E), BF16),
            pltpu.VMEM(pair + (SHARD, E), BF16),
            pltpu.VMEM(pair + (SIDE - 1, SHARD, E), BF16),
            pltpu.VMEM(pair + (SIDE, SHARD, E), BF16),
            pltpu.VMEM((SIDE, SAMPLES, E), BF16),
            pltpu.VMEM((SIDE, SAMPLES, E), BF16),
            pltpu.VMEM((SIDE, E, SAMPLES), BF16),
            pltpu.VMEM((SIDE, SAMPLES, E), BF16),
            pltpu.VMEM((GROUPS, SAMPLES, E), BF16),
            pltpu.VMEM((E, E), F32),
            pltpu.VMEM((PIECE, E), F32),
            dma((12,)),
            dma(pair), dma(pair), dma(pair), dma(pair), dma(pair), dma(pair),
            dma, dma, dma, dma((SIDE,)), dma, dma((SIDE,)), dma, dma,
        ],
        compiler_params=pltpu.CompilerParams(
            collective_id=0, has_side_effects=True, vmem_limit_bytes=32 * 1024 * 1024
        ),
        cost_estimate=pl.CostEstimate(
            flops=1_500_000_000, bytes_accessed=3_000_000, transcendentals=0
        ),
    )(*[pltpu.with_memory_space_constraint(a, pltpu.HBM) for a in inputs])
    return store(*results)


def solution(mesh):
    in_specs = (
        P("xnode", "node"),
        P("xnode", "node"),
        P("node"),
        P("node", None),
        P(None, "node", None),
        P(None, None, "node"),
        P(None, "node"),
        P("xnode", "node"),
    )
    out_specs = (P(("node", "xnode"), None), P(("node", "xnode"), None))
    return jax.shard_map(
        on_device, mesh=mesh, in_specs=in_specs, out_specs=out_specs, check_vma=False
    )
```

```python
import functools

import jax
import jax.numpy as jnp
from jax import lax
from jax.experimental import pallas as pl
from jax.experimental.pallas import tpu as pltpu
from jax.sharding import PartitionSpec as P

LAYERS = 3
SIDE = 8
CORES = 2
GROUPS = SIDE * CORES
SAMPLES = 192
RANK = 256
WIDTH = 512
FEATS = 4
E = 128
PACKED = 1024
PIECE = PACKED // GROUPS
SHARD = 48
ORDER = (4, 3, 5, 2, 6, 1, 7)
F32 = jnp.float32
BF16 = jnp.bfloat16

NN = (((1,), (0,)), ((), ()))
NT = (((1,), (1,)), ((), ()))
TN = (((0,), (0,)), ((), ()))


def dot(a, b, dims=NN):
    return lax.dot_general(a, b, dims, preferred_element_type=F32)


def kernel(
    dims_hbm, counts_hbm, pooled_hbm, proj_hbm, v_hbm, u_hbm, bias_hbm, cot_hbm,
    row_ref, pg_ref,
    dims_ref, counts_ref, pooled_ref, proj_ref, v_ref, u_ref, bias_ref, cot_ref,
    base, state, grads, ups, scale, cots, pre,
    send1, recv1, sum1, recv2, gath,
    wsend, wrecv, wturn, dsend, drecv, pgown, pgin,
    in_sem, s1_sem, r1_sem, s2_sem, r2_sem, s3_sem, r3_sem,
    ws_sem, wr_sem, ds_sem, dr_sem, fs_sem, fr_sem, ps_sem, pr_sem,
):
    node = lax.axis_index("node")
    group = lax.axis_index("xnode")
    y, z = node // SIDE, node % SIDE
    x, core = group // CORES, group % CORES
    here = (y, z)

    def along(axis, to):
        return (to * SIDE + z, group) if axis == 0 else (y * SIDE + to, group)

    def copy(src, dst, ssem, rsem, device):
        return pltpu.make_async_remote_copy(
            src_ref=src, dst_ref=dst, send_sem=ssem, recv_sem=rsem,
            device_id=device, device_id_type=pl.DeviceIdType.MESH,
        )

    barrier = pltpu.get_barrier_semaphore()
    for d in ORDER:
        for axis in (0, 1):
            to = lax.rem(here[axis] + d, SIDE)
            pl.semaphore_signal(
                barrier, inc=1, device_id=along(axis, to), device_id_type=pl.DeviceIdType.MESH
            )

    def greet_x(d, c):
        to = lax.rem(group + d, GROUPS)
        pl.semaphore_signal(
            barrier, inc=1, device_id=(node, to), device_id_type=pl.DeviceIdType.MESH
        )
        return c

    lax.fori_loop(1, GROUPS, greet_x, 0)

    pairs = {
        "dims": (dims_hbm, dims_ref),
        "counts": (counts_hbm, counts_ref),
        "pooled": (pooled_hbm, pooled_ref),
        "proj": (proj_hbm, proj_ref),
        "v0": (v_hbm.at[0], v_ref.at[0]),
        "u2": (u_hbm.at[2], u_ref.at[2]),
        "cot": (cot_hbm, cot_ref),
        "u0": (u_hbm.at[0], u_ref.at[0]),
        "v2": (v_hbm.at[2], v_ref.at[2]),
        "bias": (bias_hbm, bias_ref),
        "v1": (v_hbm.at[1], v_ref.at[1]),
        "u1": (u_hbm.at[1], u_ref.at[1]),
    }
    loads = {
        name: pltpu.make_async_copy(src, dst, in_sem.at[i])
        for i, (name, (src, dst)) in enumerate(pairs.items())
    }
    for load in loads.values():
        load.start()

    loads["dims"].wait()
    ends = []
    total = jnp.int32(0)
    for j in range(FEATS):
        total = total + dims_ref[j]
        ends.append(total)
    starts = [jnp.int32(0)] + ends[:-1]

    def inside(c, j):
        return jnp.where((starts[j] <= c * E) & (ends[j] > c * E), 1.0, 0.0)

    def pick(c, parts):
        spot = jnp.full((SAMPLES, E), c * E, jnp.int32)
        out = parts[0]
        for j in range(1, FEATS):
            out = jnp.where(spot >= starts[j], parts[j], out)
        return out

    loads["counts"].wait()
    counts = counts_ref[...].astype(F32).astype(BF16)
    lane = lax.broadcasted_iota(jnp.int32, (FEATS, WIDTH), 1)
    first = lax.broadcasted_iota(jnp.int32, (FEATS, WIDTH), 0) * E
    spread = jnp.where((lane >= first) & (lane < first + E), 1.0, 0.0).astype(BF16)
    scale[...] = dot(counts, spread, TN)
    loads["pooled"].wait()
    loads["proj"].wait()
    blocks = [
        dot(pooled_ref[:, c * E : (c + 1) * E], proj_ref[c * E : (c + 1) * E, :])
        for c in range(SIDE)
    ]
    for j in range(FEATS):
        own = slice(j * E, (j + 1) * E)
        start = jnp.zeros((SAMPLES, E), F32)
        for c in range(SIDE):
            start = start + inside(c, j) * blocks[c]
        start = jnp.where(scale[:, own] > 0, start, 0.0).astype(BF16)
        base[:, own] = start
        state[:, own] = start.astype(F32)

    def start1(r, k, partial):
        rounded = partial.astype(BF16)
        for i in range(SIDE):
            a, b = i % 4, i // 4
            send1[r, k, i] = rounded[a * SHARD : (a + 1) * SHARD, b * E : (b + 1) * E]
        if r == 0 and k == 0:
            pl.semaphore_wait(barrier, 2 * (SIDE - 1) + GROUPS - 1)
        for d in ORDER:
            to = lax.rem(here[k] + d, SIDE)
            copy(
                send1.at[r, k, to], recv1.at[r, k, d - 1], s1_sem.at[r, k], r1_sem.at[r, k],
                along(k, to),
            ).start()

    def settle(ref, sem):
        pltpu.make_async_copy(ref, ref, sem).wait()

    def start2(r, k):
        settle(recv1.at[r, k], r1_sem.at[r, k])
        acc = send1[r, k, here[k]].astype(F32)
        for d in range(SIDE - 1):
            acc = acc + recv1[r, k, d].astype(F32)
        sum1[r, k] = acc.astype(BF16)
        for d in ORDER:
            to = lax.rem(here[1 - k] + d, SIDE)
            copy(
                sum1.at[r, k], recv2.at[r, k, d - 1], s2_sem.at[r, k], r2_sem.at[r, k],
                along(1 - k, to),
            ).start()

    def start3(r, k):
        settle(recv2.at[r, k], r2_sem.at[r, k])
        acc = sum1[r, k].astype(F32)
        for d in range(SIDE - 1):
            acc = acc + recv2[r, k, d].astype(F32)
        mine = gath.at[r, k, here[k]]
        gath[r, k, here[k]] = acc.astype(BF16)
        for d in ORDER:
            to = lax.rem(here[k] + d, SIDE)
            copy(mine, mine, s3_sem.at[r, k], r3_sem.at[r, k], along(k, to)).start()

    def finish(r, k):
        settle(recv1.at[r, k], r3_sem.at[r, k])
        whole = gath[r, k]
        return jnp.concatenate(
            [whole[0:4].reshape(SAMPLES, E), whole[4:8].reshape(SAMPLES, E)], axis=1
        )

    def start_forward(r):
        start1(r, 0, dot(state[...].astype(BF16), v_ref[r]))

    def start_backward(r):
        product = (grads[r] * base[...].astype(F32)).astype(BF16)
        start1(r, 1, dot(product, u_ref[LAYERS - 1 - r], NT))

    def share_w():
        column = lax.broadcasted_iota(jnp.int32, (FEATS, PACKED), 1)
        row = lax.broadcasted_iota(jnp.int32, (FEATS, PACKED), 0)
        low = jnp.zeros((FEATS, PACKED), jnp.int32)
        high = low
        for j in range(FEATS):
            low = jnp.where(row == j, starts[j], low)
            high = jnp.where(row == j, ends[j], high)
        member = jnp.where((column >= low) & (column < high), 1.0, 0.0).astype(BF16)
        weight = dot(counts, member, TN)
        for c in range(SIDE):
            own = slice(c * E, (c + 1) * E)
            wsend[c] = (pooled_ref[:, own].astype(F32) * weight[:, own]).astype(BF16)
        for d in ORDER:
            to = lax.rem(x + d, SIDE)
            copy(
                wsend.at[to], wrecv.at[x], ws_sem, wr_sem, (node, to * CORES + core)
            ).start()
        wrecv[x] = wsend[x]

    loads["v0"].wait()
    start_forward(0)
    loads["cot"].wait()
    grads[0] = cot_ref[...].astype(F32)
    loads["u2"].wait()
    start_backward(0)

    wide = scale[...]
    scale[...] = jnp.where(wide > 0, 1.0, 0.0) / jnp.maximum(wide, 1.0)
    for name in ("u0", "v2", "bias", "v1", "u1"):
        loads[name].wait()

    for r in range(LAYERS):
        last = r == LAYERS - 1
        start2(r, 0)
        start2(r, 1)
        if r == 0:
            share_w()
        start3(r, 0)
        start3(r, 1)
        if r == 1:
            settle(wrecv.at[0 : SIDE - 1], wr_sem)
            for c in range(SIDE):
                wturn[c] = wrecv[c].T
        if last:
            cot = grads[0]
            pre[...] = scale[...] * (
                grads[1] * ups[1] + grads[2] * ups[0] + grads[2] + cot * bias_ref[2:3, :]
            )
            cots[...] = scale[...] * cot
        up = dot(finish(r, 0), u_ref[r])
        if last:
            pre[...] = pre[...] + cots[...] * up
        else:
            up = up + bias_ref[r : r + 1, :]
            ups[r] = up
            state[...] = base[...].astype(F32) * up + state[...]
            start_forward(r + 1)
        down = dot(finish(r, 1), v_ref[LAYERS - 1 - r], NT)
        if last:
            pre[...] = pre[...] + scale[...] * down
        else:
            grads[r + 1] = grads[r] + down
            start_backward(r + 1)

    parts = [pre[:, j * E : (j + 1) * E] for j in range(FEATS)]
    for c in range(SIDE):
        dsend[c] = pick(c, parts).astype(BF16)
    for d in ORDER:
        to = lax.rem(x + d, SIDE)
        copy(
            dsend.at[to], drecv.at[group], ds_sem, dr_sem.at[d], (node, to * CORES + core)
        ).start()
    sibling = (node, x * CORES + 1 - core)
    copy(dsend.at[x], drecv.at[group], fs_sem, fr_sem.at[0], sibling).start()
    drecv[group] = dsend[x]

    for r in range(LAYERS):
        for k in range(2):
            settle(recv1.at[r, k], s1_sem.at[r, k])
            settle(recv1.at[r, k], s2_sem.at[r, k])
            settle(recv1.at[r, k], s3_sem.at[r, k])
    settle(wrecv.at[0 : SIDE - 1], ws_sem)

    mine = proj_ref[pl.ds(pl.multiple_of(group * PIECE, PIECE), PIECE), :]
    half = pl.ds(pl.multiple_of(core * PIECE, PIECE), PIECE)
    other = pl.ds(pl.multiple_of((1 - core) * PIECE, PIECE), PIECE)

    def use(d):
        chip = lax.rem(x + SIDE - d, SIDE)
        settle(drecv.at[chip * CORES + 1 - core], fr_sem.at[d])
        pair = drecv[pl.ds(chip * CORES, CORES)].reshape(CORES * SAMPLES, E)
        at = pl.ds(pl.multiple_of(chip * (CORES * SAMPLES), CORES * SAMPLES), CORES * SAMPLES)
        row_ref[:, at] = dot(mine, pair, NT).astype(BF16)

    pgown[...] = dot(wturn[x], dsend[x])
    waiting = [0]
    for d in ORDER:
        chip = lax.rem(x + SIDE - d, SIDE)
        block = drecv.at[chip * CORES + core]
        settle(block, dr_sem.at[d])
        copy(block, block, fs_sem, fr_sem.at[d], sibling).start()
        pgown[...] = pgown[...] + dot(wturn[chip], block[...])
        waiting.append(d)
        if d == ORDER[-1]:
            parting = copy(pgown.at[other], pgin, ps_sem, pr_sem, sibling)
            parting.start()
        if len(waiting) > 2:
            use(waiting.pop(0))
    for d in waiting:
        use(d)
    parting.wait()
    pg_ref[...] = pgown[half, :] + pgin[...]
    settle(drecv.at[0 : SIDE - 1], ds_sem)
    settle(drecv.at[0:SIDE], fs_sem)


def store_kernel(row_ref, pg_ref, row_out, pg_out, sems):
    moves = [
        pltpu.make_async_copy(row_ref, row_out, sems.at[0]),
        pltpu.make_async_copy(pg_ref, pg_out, sems.at[1]),
    ]
    for move in moves:
        move.start()
    for move in moves:
        move.wait()


def store(row_grads, proj_grad):
    here = pl.BlockSpec(memory_space=pl.ANY)
    return pl.pallas_call(
        store_kernel,
        out_shape=(
            pltpu.HBM(row_grads.shape, row_grads.dtype),
            pltpu.HBM(proj_grad.shape, proj_grad.dtype),
        ),
        in_specs=[here, here],
        out_specs=(here, here),
        scratch_shapes=[pltpu.SemaphoreType.DMA((2,))],
        compiler_params=pltpu.CompilerParams(vmem_limit_bytes=4 * 1024 * 1024),
    )(*[pltpu.with_memory_space_constraint(a, pltpu.VMEM) for a in (row_grads, proj_grad)])


def on_device(pooled, counts, dims, proj, v_weight, u_weight, bias, cotangent):
    vmem = pl.BlockSpec(memory_space=pltpu.VMEM)
    hbm = pl.BlockSpec(memory_space=pl.ANY)
    dma = pltpu.SemaphoreType.DMA
    pair = (LAYERS, 2)
    inputs = (dims, counts.T, pooled, proj, v_weight, u_weight, bias, cotangent)
    results = pl.pallas_call(
        kernel,
        out_shape=(
            jax.ShapeDtypeStruct((PIECE, GROUPS * SAMPLES), BF16),
            jax.ShapeDtypeStruct((PIECE, E), F32),
        ),
        in_specs=[hbm] * 8,
        out_specs=(vmem, vmem),
        scratch_shapes=[pltpu.SMEM(dims.shape, dims.dtype)]
        + [pltpu.VMEM(a.shape, a.dtype) for a in inputs[1:]]
        + [
            pltpu.VMEM((SAMPLES, WIDTH), BF16),
            pltpu.VMEM((SAMPLES, WIDTH), F32),
            pltpu.VMEM((LAYERS, SAMPLES, WIDTH), F32),
            pltpu.VMEM((LAYERS - 1, SAMPLES, WIDTH), F32),
            pltpu.VMEM((SAMPLES, WIDTH), F32),
            pltpu.VMEM((SAMPLES, WIDTH), F32),
            pltpu.VMEM((SAMPLES, WIDTH), F32),
            pltpu.VMEM(pair + (SIDE, SHARD, E), BF16),
            pltpu.VMEM(pair + (SIDE - 1, SHARD, E), BF16),
            pltpu.VMEM(pair + (SHARD, E), BF16),
            pltpu.VMEM(pair + (SIDE - 1, SHARD, E), BF16),
            pltpu.VMEM(pair + (SIDE, SHARD, E), BF16),
            pltpu.VMEM((SIDE, SAMPLES, E), BF16),
            pltpu.VMEM((SIDE, SAMPLES, E), BF16),
            pltpu.VMEM((SIDE, E, SAMPLES), BF16),
            pltpu.VMEM((SIDE, SAMPLES, E), BF16),
            pltpu.VMEM((GROUPS, SAMPLES, E), BF16),
            pltpu.VMEM((E, E), F32),
            pltpu.VMEM((PIECE, E), F32),
            dma((12,)),
            dma(pair), dma(pair), dma(pair), dma(pair), dma(pair), dma(pair),
            dma, dma, dma, dma((SIDE,)), dma, dma((SIDE,)), dma, dma,
        ],
        compiler_params=pltpu.CompilerParams(
            collective_id=0, has_side_effects=True, vmem_limit_bytes=32 * 1024 * 1024
        ),
        cost_estimate=pl.CostEstimate(
            flops=1_500_000_000, bytes_accessed=3_000_000, transcendentals=0
        ),
    )(*[pltpu.with_memory_space_constraint(a, pltpu.HBM) for a in inputs])
    return store(*results)


def solution(mesh):
    in_specs = (
        P("xnode", "node"),
        P("xnode", "node"),
        P("node"),
        P("node", None),
        P(None, "node", None),
        P(None, None, "node"),
        P(None, "node"),
        P("xnode", "node"),
    )
    out_specs = (P(("node", "xnode"), None), P(("node", "xnode"), None))
    return jax.shard_map(
        on_device, mesh=mesh, in_specs=in_specs, out_specs=out_specs, check_vma=False
    )
```

```python
import functools

import jax
import jax.numpy as jnp
from jax import lax
from jax.experimental import pallas as pl
from jax.experimental.pallas import tpu as pltpu
from jax.sharding import PartitionSpec as P

LAYERS = 3
SIDE = 8
CORES = 2
GROUPS = SIDE * CORES
SAMPLES = 192
RANK = 256
WIDTH = 512
FEATS = 4
E = 128
PACKED = 1024
PIECE = PACKED // GROUPS
SHARD = 48
XORDER = (4, 1, 7, 3, 5, 2, 6)
ORDER = (4, 3, 5, 2, 6, 1, 7)
F32 = jnp.float32
BF16 = jnp.bfloat16

NN = (((1,), (0,)), ((), ()))
NT = (((1,), (1,)), ((), ()))
TN = (((0,), (0,)), ((), ()))


def dot(a, b, dims=NN):
    return lax.dot_general(a, b, dims, preferred_element_type=F32)


def kernel(
    dims_hbm, counts_hbm, pooled_hbm, proj_hbm, v_hbm, u_hbm, bias_hbm, cot_hbm,
    row_ref, pg_ref,
    dims_ref, counts_ref, pooled_ref, proj_ref, v_ref, u_ref, bias_ref, cot_ref,
    base, state, grads, ups, scale, cots, pre,
    send1, recv1, sum1, recv2, gath,
    wsend, wrecv, wturn, dsend, drecv, pgown, pgin,
    in_sem, s1_sem, r1_sem, s2_sem, r2_sem, s3_sem, r3_sem,
    ws_sem, wr_sem, ds_sem, dr_sem, fs_sem, fr_sem, ps_sem, pr_sem,
):
    node = lax.axis_index("node")
    group = lax.axis_index("xnode")
    y, z = node // SIDE, node % SIDE
    x, core = group // CORES, group % CORES
    here = (y, z)

    def along(axis, to):
        return (to * SIDE + z, group) if axis == 0 else (y * SIDE + to, group)

    def copy(src, dst, ssem, rsem, device):
        return pltpu.make_async_remote_copy(
            src_ref=src, dst_ref=dst, send_sem=ssem, recv_sem=rsem,
            device_id=device, device_id_type=pl.DeviceIdType.MESH,
        )

    barrier = pltpu.get_barrier_semaphore()
    sibling = (node, x * CORES + 1 - core)

    def greet(device):
        pl.semaphore_signal(
            barrier, inc=1, device_id=device, device_id_type=pl.DeviceIdType.MESH
        )

    for d in ORDER:
        for axis in (0, 1):
            greet(along(axis, lax.rem(here[axis] + d, SIDE)))
        greet((node, lax.rem(x + d, SIDE) * CORES + core))
    greet(sibling)

    pairs = {
        "dims": (dims_hbm, dims_ref),
        "counts": (counts_hbm, counts_ref),
        "pooled": (pooled_hbm, pooled_ref),
        "proj": (proj_hbm, proj_ref),
        "v0": (v_hbm.at[0], v_ref.at[0]),
        "u2": (u_hbm.at[2], u_ref.at[2]),
        "cot": (cot_hbm, cot_ref),
        "u0": (u_hbm.at[0], u_ref.at[0]),
        "v2": (v_hbm.at[2], v_ref.at[2]),
        "bias": (bias_hbm, bias_ref),
        "v1": (v_hbm.at[1], v_ref.at[1]),
        "u1": (u_hbm.at[1], u_ref.at[1]),
    }
    loads = {
        name: pltpu.make_async_copy(src, dst, in_sem.at[i])
        for i, (name, (src, dst)) in enumerate(pairs.items())
    }
    for load in loads.values():
        load.start()

    loads["dims"].wait()
    ends = []
    total = jnp.int32(0)
    for j in range(FEATS):
        total = total + dims_ref[j]
        ends.append(total)
    starts = [jnp.int32(0)] + ends[:-1]

    def inside(c, j):
        return jnp.where((starts[j] <= c * E) & (ends[j] > c * E), 1.0, 0.0)

    def pick(c, parts):
        spot = jnp.full((SAMPLES, E), c * E, jnp.int32)
        out = parts[0]
        for j in range(1, FEATS):
            out = jnp.where(spot >= starts[j], parts[j], out)
        return out

    loads["counts"].wait()
    counts = counts_ref[...].astype(F32).astype(BF16)
    lane = lax.broadcasted_iota(jnp.int32, (FEATS, WIDTH), 1)
    first = lax.broadcasted_iota(jnp.int32, (FEATS, WIDTH), 0) * E
    spread = jnp.where((lane >= first) & (lane < first + E), 1.0, 0.0).astype(BF16)
    scale[...] = dot(counts, spread, TN)
    loads["pooled"].wait()
    loads["proj"].wait()
    blocks = [
        dot(pooled_ref[:, c * E : (c + 1) * E], proj_ref[c * E : (c + 1) * E, :])
        for c in range(SIDE)
    ]
    for j in range(FEATS):
        own = slice(j * E, (j + 1) * E)
        start = jnp.zeros((SAMPLES, E), F32)
        for c in range(SIDE):
            start = start + inside(c, j) * blocks[c]
        start = jnp.where(scale[:, own] > 0, start, 0.0).astype(BF16)
        base[:, own] = start
        state[:, own] = start.astype(F32)

    def start1(r, k, partial):
        rounded = partial.astype(BF16)
        for i in range(SIDE):
            a, b = i % 4, i // 4
            send1[r, k, i] = rounded[a * SHARD : (a + 1) * SHARD, b * E : (b + 1) * E]
        if r == 0 and k == 0:
            pl.semaphore_wait(barrier, 3 * (SIDE - 1) + 1)
        for d in ORDER:
            to = lax.rem(here[k] + d, SIDE)
            copy(
                send1.at[r, k, to], recv1.at[r, k, d - 1], s1_sem.at[r, k], r1_sem.at[r, k],
                along(k, to),
            ).start()

    def settle(ref, sem):
        pltpu.make_async_copy(ref, ref, sem).wait()

    def start2(r, k):
        settle(recv1.at[r, k], r1_sem.at[r, k])
        acc = send1[r, k, here[k]].astype(F32)
        for d in range(SIDE - 1):
            acc = acc + recv1[r, k, d].astype(F32)
        sum1[r, k] = acc.astype(BF16)
        for d in ORDER:
            to = lax.rem(here[1 - k] + d, SIDE)
            copy(
                sum1.at[r, k], recv2.at[r, k, d - 1], s2_sem.at[r, k], r2_sem.at[r, k],
                along(1 - k, to),
            ).start()

    def start3(r, k):
        settle(recv2.at[r, k], r2_sem.at[r, k])
        acc = sum1[r, k].astype(F32)
        for d in range(SIDE - 1):
            acc = acc + recv2[r, k, d].astype(F32)
        mine = gath.at[r, k, here[k]]
        gath[r, k, here[k]] = acc.astype(BF16)
        for d in ORDER:
            to = lax.rem(here[k] + d, SIDE)
            copy(mine, mine, s3_sem.at[r, k], r3_sem.at[r, k], along(k, to)).start()

    def finish(r, k):
        settle(recv1.at[r, k], r3_sem.at[r, k])
        whole = gath[r, k]
        return jnp.concatenate(
            [whole[0:4].reshape(SAMPLES, E), whole[4:8].reshape(SAMPLES, E)], axis=1
        )

    def start_forward(r):
        start1(r, 0, dot(state[...].astype(BF16), v_ref[r]))

    def start_backward(r):
        product = (grads[r] * base[...].astype(F32)).astype(BF16)
        start1(r, 1, dot(product, u_ref[LAYERS - 1 - r], NT))

    def share_w():
        column = lax.broadcasted_iota(jnp.int32, (FEATS, PACKED), 1)
        row = lax.broadcasted_iota(jnp.int32, (FEATS, PACKED), 0)
        low = jnp.zeros((FEATS, PACKED), jnp.int32)
        high = low
        for j in range(FEATS):
            low = jnp.where(row == j, starts[j], low)
            high = jnp.where(row == j, ends[j], high)
        member = jnp.where((column >= low) & (column < high), 1.0, 0.0).astype(BF16)
        weight = dot(counts, member, TN)
        for c in range(SIDE):
            own = slice(c * E, (c + 1) * E)
            wsend[c] = (pooled_ref[:, own].astype(F32) * weight[:, own]).astype(BF16)
        for d in ORDER:
            to = lax.rem(x + d, SIDE)
            copy(
                wsend.at[to], wrecv.at[x], ws_sem, wr_sem, (node, to * CORES + core)
            ).start()
        wrecv[x] = wsend[x]

    loads["v0"].wait()
    start_forward(0)
    loads["cot"].wait()
    grads[0] = cot_ref[...].astype(F32)
    loads["u2"].wait()
    start_backward(0)

    wide = scale[...]
    scale[...] = jnp.where(wide > 0, 1.0, 0.0) / jnp.maximum(wide, 1.0)
    for name in ("u0", "v2", "bias", "v1", "u1"):
        loads[name].wait()

    for r in range(LAYERS):
        last = r == LAYERS - 1
        start2(r, 0)
        start2(r, 1)
        if r == 0:
            share_w()
        start3(r, 0)
        start3(r, 1)
        if r == 1:
            settle(wrecv.at[0 : SIDE - 1], wr_sem)
            for c in range(SIDE):
                wturn[c] = wrecv[c].T
        if last:
            cot = grads[0]
            pre[...] = scale[...] * (
                grads[1] * ups[1] + grads[2] * ups[0] + grads[2] + cot * bias_ref[2:3, :]
            )
            cots[...] = scale[...] * cot
        up = dot(finish(r, 0), u_ref[r])
        if last:
            pre[...] = pre[...] + cots[...] * up
        else:
            up = up + bias_ref[r : r + 1, :]
            ups[r] = up
            state[...] = base[...].astype(F32) * up + state[...]
            start_forward(r + 1)
        down = dot(finish(r, 1), v_ref[LAYERS - 1 - r], NT)
        if last:
            pre[...] = pre[...] + scale[...] * down
        else:
            grads[r + 1] = grads[r] + down
            start_backward(r + 1)

    parts = [pre[:, j * E : (j + 1) * E] for j in range(FEATS)]
    for c in range(SIDE):
        dsend[c] = pick(c, parts).astype(BF16)
    for d in XORDER:
        to = lax.rem(x + d, SIDE)
        copy(
            dsend.at[to], drecv.at[group], ds_sem, dr_sem.at[d], (node, to * CORES + core)
        ).start()
    copy(dsend.at[x], drecv.at[group], fs_sem, fr_sem.at[0], sibling).start()
    drecv[group] = dsend[x]

    for r in range(LAYERS):
        for k in range(2):
            settle(recv1.at[r, k], s1_sem.at[r, k])
            settle(recv1.at[r, k], s2_sem.at[r, k])
            settle(recv1.at[r, k], s3_sem.at[r, k])
    settle(wrecv.at[0 : SIDE - 1], ws_sem)

    mine = proj_ref[pl.ds(pl.multiple_of(group * PIECE, PIECE), PIECE), :]
    half = pl.ds(pl.multiple_of(core * PIECE, PIECE), PIECE)
    other = pl.ds(pl.multiple_of((1 - core) * PIECE, PIECE), PIECE)

    def use(d):
        chip = lax.rem(x + SIDE - d, SIDE)
        settle(drecv.at[chip * CORES + 1 - core], fr_sem.at[d])
        pair = drecv[pl.ds(chip * CORES, CORES)].reshape(CORES * SAMPLES, E)
        at = pl.ds(pl.multiple_of(chip * (CORES * SAMPLES), CORES * SAMPLES), CORES * SAMPLES)
        row_ref[:, at] = dot(mine, pair, NT).astype(BF16)

    pgown[...] = dot(wturn[x], dsend[x])
    waiting = [0]
    for d in XORDER:
        chip = lax.rem(x + SIDE - d, SIDE)
        block = drecv.at[chip * CORES + core]
        settle(block, dr_sem.at[d])
        copy(block, block, fs_sem, fr_sem.at[d], sibling).start()
        pgown[...] = pgown[...] + dot(wturn[chip], block[...])
        waiting.append(d)
        if d == XORDER[-1]:
            parting = copy(pgown.at[other], pgin, ps_sem, pr_sem, sibling)
            parting.start()
        if len(waiting) > 4:
            use(waiting.pop(0))
    for d in waiting:
        use(d)
    parting.wait()
    pg_ref[...] = pgown[half, :] + pgin[...]
    settle(drecv.at[0 : SIDE - 1], ds_sem)
    settle(drecv.at[0:SIDE], fs_sem)


def store_kernel(row_ref, pg_ref, row_out, pg_out, sems):
    moves = [pltpu.make_async_copy(pg_ref, pg_out, sems.at[0])]
    for i in range(4):
        rows = pl.ds(i * 16, 16)
        moves.append(
            pltpu.make_async_copy(row_ref.at[rows], row_out.at[rows], sems.at[i + 1])
        )
    for move in moves:
        move.start()
    for move in moves:
        move.wait()


def store(row_grads, proj_grad):
    here = pl.BlockSpec(memory_space=pl.ANY)
    return pl.pallas_call(
        store_kernel,
        out_shape=(
            pltpu.HBM(row_grads.shape, row_grads.dtype),
            pltpu.HBM(proj_grad.shape, proj_grad.dtype),
        ),
        in_specs=[here, here],
        out_specs=(here, here),
        scratch_shapes=[pltpu.SemaphoreType.DMA((5,))],
        compiler_params=pltpu.CompilerParams(vmem_limit_bytes=4 * 1024 * 1024),
    )(*[pltpu.with_memory_space_constraint(a, pltpu.VMEM) for a in (row_grads, proj_grad)])


def on_device(pooled, counts, dims, proj, v_weight, u_weight, bias, cotangent):
    vmem = pl.BlockSpec(memory_space=pltpu.VMEM)
    hbm = pl.BlockSpec(memory_space=pl.ANY)
    dma = pltpu.SemaphoreType.DMA
    pair = (LAYERS, 2)
    inputs = (dims, counts.T, pooled, proj, v_weight, u_weight, bias, cotangent)
    results = pl.pallas_call(
        kernel,
        out_shape=(
            jax.ShapeDtypeStruct((PIECE, GROUPS * SAMPLES), BF16),
            jax.ShapeDtypeStruct((PIECE, E), F32),
        ),
        in_specs=[hbm] * 8,
        out_specs=(vmem, vmem),
        scratch_shapes=[pltpu.SMEM(dims.shape, dims.dtype)]
        + [pltpu.VMEM(a.shape, a.dtype) for a in inputs[1:]]
        + [
            pltpu.VMEM((SAMPLES, WIDTH), BF16),
            pltpu.VMEM((SAMPLES, WIDTH), F32),
            pltpu.VMEM((LAYERS, SAMPLES, WIDTH), F32),
            pltpu.VMEM((LAYERS - 1, SAMPLES, WIDTH), F32),
            pltpu.VMEM((SAMPLES, WIDTH), F32),
            pltpu.VMEM((SAMPLES, WIDTH), F32),
            pltpu.VMEM((SAMPLES, WIDTH), F32),
            pltpu.VMEM(pair + (SIDE, SHARD, E), BF16),
            pltpu.VMEM(pair + (SIDE - 1, SHARD, E), BF16),
            pltpu.VMEM(pair + (SHARD, E), BF16),
            pltpu.VMEM(pair + (SIDE - 1, SHARD, E), BF16),
            pltpu.VMEM(pair + (SIDE, SHARD, E), BF16),
            pltpu.VMEM((SIDE, SAMPLES, E), BF16),
            pltpu.VMEM((SIDE, SAMPLES, E), BF16),
            pltpu.VMEM((SIDE, E, SAMPLES), BF16),
            pltpu.VMEM((SIDE, SAMPLES, E), BF16),
            pltpu.VMEM((GROUPS, SAMPLES, E), BF16),
            pltpu.VMEM((E, E), F32),
            pltpu.VMEM((PIECE, E), F32),
            dma((12,)),
            dma(pair), dma(pair), dma(pair), dma(pair), dma(pair), dma(pair),
            dma, dma, dma, dma((SIDE,)), dma, dma((SIDE,)), dma, dma,
        ],
        compiler_params=pltpu.CompilerParams(
            collective_id=0, has_side_effects=True, vmem_limit_bytes=32 * 1024 * 1024
        ),
        cost_estimate=pl.CostEstimate(
            flops=1_500_000_000, bytes_accessed=3_000_000, transcendentals=0
        ),
    )(*[pltpu.with_memory_space_constraint(a, pltpu.HBM) for a in inputs])
    return store(*results)


def solution(mesh):
    in_specs = (
        P("xnode", "node"),
        P("xnode", "node"),
        P("node"),
        P("node", None),
        P(None, "node", None),
        P(None, None, "node"),
        P(None, "node"),
        P("xnode", "node"),
    )
    out_specs = (P(("node", "xnode"), None), P(("node", "xnode"), None))
    return jax.shard_map(
        on_device, mesh=mesh, in_specs=in_specs, out_specs=out_specs, check_vma=False
    )
```

```python
import functools

import jax
import jax.numpy as jnp
from jax import lax
from jax.experimental import pallas as pl
from jax.experimental.pallas import tpu as pltpu
from jax.sharding import PartitionSpec as P

LAYERS = 3
SIDE = 8
CORES = 2
GROUPS = SIDE * CORES
SAMPLES = 192
RANK = 256
WIDTH = 512
FEATS = 4
E = 128
PACKED = 1024
PIECE = PACKED // GROUPS
SHARD = 48
XORDER = (4, 1, 7, 3, 5, 2, 6)
ORDER = (4, 3, 5, 2, 6, 1, 7)
F32 = jnp.float32
BF16 = jnp.bfloat16

NN = (((1,), (0,)), ((), ()))
NT = (((1,), (1,)), ((), ()))
TN = (((0,), (0,)), ((), ()))


def dot(a, b, dims=NN):
    return lax.dot_general(a, b, dims, preferred_element_type=F32)


def kernel(
    dims_hbm, counts_hbm, pooled_hbm, proj_hbm, v_hbm, u_hbm, bias_hbm, cot_hbm,
    row_ref, pg_ref,
    dims_ref, counts_ref, pooled_ref, proj_ref, v_ref, u_ref, bias_ref, cot_ref,
    base, state, grads, ups, scale, cots, pre,
    send1, recv1, sum1, recv2, gath,
    wsend, wrecv, wturn, dsend, drecv, pgown, pgin,
    in_sem, s1_sem, r1_sem, s2_sem, r2_sem, s3_sem, r3_sem,
    ws_sem, wr_sem, ds_sem, dr_sem, fs_sem, fr_sem, ps_sem, pr_sem,
):
    node = lax.axis_index("node")
    group = lax.axis_index("xnode")
    y, z = node // SIDE, node % SIDE
    x, core = group // CORES, group % CORES
    here = (y, z)

    def along(axis, to):
        return (to * SIDE + z, group) if axis == 0 else (y * SIDE + to, group)

    def copy(src, dst, ssem, rsem, device):
        return pltpu.make_async_remote_copy(
            src_ref=src, dst_ref=dst, send_sem=ssem, recv_sem=rsem,
            device_id=device, device_id_type=pl.DeviceIdType.MESH,
        )

    barrier = pltpu.get_barrier_semaphore()
    sibling = (node, x * CORES + 1 - core)

    def greet(device):
        pl.semaphore_signal(
            barrier, inc=1, device_id=device, device_id_type=pl.DeviceIdType.MESH
        )

    for d in ORDER:
        for axis in (0, 1):
            greet(along(axis, lax.rem(here[axis] + d, SIDE)))
        greet((node, lax.rem(x + d, SIDE) * CORES + core))
    greet(sibling)

    pairs = {
        "dims": (dims_hbm, dims_ref),
        "counts": (counts_hbm, counts_ref),
        "pooled": (pooled_hbm, pooled_ref),
        "proj": (proj_hbm, proj_ref),
        "v0": (v_hbm.at[0], v_ref.at[0]),
        "u2": (u_hbm.at[2], u_ref.at[2]),
        "cot": (cot_hbm, cot_ref),
        "u0": (u_hbm.at[0], u_ref.at[0]),
        "v2": (v_hbm.at[2], v_ref.at[2]),
        "bias": (bias_hbm, bias_ref),
        "v1": (v_hbm.at[1], v_ref.at[1]),
        "u1": (u_hbm.at[1], u_ref.at[1]),
    }
    loads = {
        name: pltpu.make_async_copy(src, dst, in_sem.at[i])
        for i, (name, (src, dst)) in enumerate(pairs.items())
    }
    for load in loads.values():
        load.start()

    loads["dims"].wait()
    ends = []
    total = jnp.int32(0)
    for j in range(FEATS):
        total = total + dims_ref[j]
        ends.append(total)
    starts = [jnp.int32(0)] + ends[:-1]

    def inside(c, j):
        return jnp.where((starts[j] <= c * E) & (ends[j] > c * E), 1.0, 0.0)

    def pick(c, parts):
        spot = jnp.full((SAMPLES, E), c * E, jnp.int32)
        out = parts[0]
        for j in range(1, FEATS):
            out = jnp.where(spot >= starts[j], parts[j], out)
        return out

    loads["counts"].wait()
    counts = counts_ref[...].astype(F32).astype(BF16)
    lane = lax.broadcasted_iota(jnp.int32, (FEATS, WIDTH), 1)
    first = lax.broadcasted_iota(jnp.int32, (FEATS, WIDTH), 0) * E
    spread = jnp.where((lane >= first) & (lane < first + E), 1.0, 0.0).astype(BF16)
    scale[...] = dot(counts, spread, TN)
    loads["pooled"].wait()
    loads["proj"].wait()
    blocks = [
        dot(pooled_ref[:, c * E : (c + 1) * E], proj_ref[c * E : (c + 1) * E, :])
        for c in range(SIDE)
    ]
    for j in range(FEATS):
        own = slice(j * E, (j + 1) * E)
        start = jnp.zeros((SAMPLES, E), F32)
        for c in range(SIDE):
            start = start + inside(c, j) * blocks[c]
        start = jnp.where(scale[:, own] > 0, start, 0.0).astype(BF16)
        base[:, own] = start
        state[:, own] = start.astype(F32)

    def start1(r, k, partial):
        rounded = partial.astype(BF16)
        for i in range(SIDE):
            a, b = i % 4, i // 4
            send1[r, k, i] = rounded[a * SHARD : (a + 1) * SHARD, b * E : (b + 1) * E]
        if r == 0 and k == 0:
            pl.semaphore_wait(barrier, 3 * (SIDE - 1) + 1)
        for d in ORDER:
            to = lax.rem(here[k] + d, SIDE)
            copy(
                send1.at[r, k, to], recv1.at[r, k, d - 1], s1_sem.at[r, k], r1_sem.at[r, k],
                along(k, to),
            ).start()

    def settle(ref, sem):
        pltpu.make_async_copy(ref, ref, sem).wait()

    def start2(r, k):
        settle(recv1.at[r, k], r1_sem.at[r, k])
        acc = send1[r, k, here[k]].astype(F32)
        for d in range(SIDE - 1):
            acc = acc + recv1[r, k, d].astype(F32)
        sum1[r, k] = acc.astype(BF16)
        for d in ORDER:
            to = lax.rem(here[1 - k] + d, SIDE)
            copy(
                sum1.at[r, k], recv2.at[r, k, d - 1], s2_sem.at[r, k], r2_sem.at[r, k],
                along(1 - k, to),
            ).start()

    def start3(r, k):
        settle(recv2.at[r, k], r2_sem.at[r, k])
        acc = sum1[r, k].astype(F32)
        for d in range(SIDE - 1):
            acc = acc + recv2[r, k, d].astype(F32)
        mine = gath.at[r, k, here[k]]
        gath[r, k, here[k]] = acc.astype(BF16)
        for d in ORDER:
            to = lax.rem(here[k] + d, SIDE)
            copy(mine, mine, s3_sem.at[r, k], r3_sem.at[r, k], along(k, to)).start()

    def finish(r, k):
        settle(recv1.at[r, k], r3_sem.at[r, k])
        whole = gath[r, k]
        return jnp.concatenate(
            [whole[0:4].reshape(SAMPLES, E), whole[4:8].reshape(SAMPLES, E)], axis=1
        )

    def start_forward(r):
        start1(r, 0, dot(state[...].astype(BF16), v_ref[r]))

    def start_backward(r):
        product = (grads[r] * base[...].astype(F32)).astype(BF16)
        start1(r, 1, dot(product, u_ref[LAYERS - 1 - r], NT))

    def share_w():
        column = lax.broadcasted_iota(jnp.int32, (FEATS, PACKED), 1)
        row = lax.broadcasted_iota(jnp.int32, (FEATS, PACKED), 0)
        low = jnp.zeros((FEATS, PACKED), jnp.int32)
        high = low
        for j in range(FEATS):
            low = jnp.where(row == j, starts[j], low)
            high = jnp.where(row == j, ends[j], high)
        member = jnp.where((column >= low) & (column < high), 1.0, 0.0).astype(BF16)
        weight = dot(counts, member, TN)
        for c in range(SIDE):
            own = slice(c * E, (c + 1) * E)
            wsend[c] = (pooled_ref[:, own].astype(F32) * weight[:, own]).astype(BF16)
        for d in ORDER:
            to = lax.rem(x + d, SIDE)
            copy(
                wsend.at[to], wrecv.at[x], ws_sem, wr_sem, (node, to * CORES + core)
            ).start()
        wrecv[x] = wsend[x]

    loads["v0"].wait()
    start_forward(0)
    loads["cot"].wait()
    grads[0] = cot_ref[...].astype(F32)
    loads["u2"].wait()
    start_backward(0)

    wide = scale[...]
    scale[...] = jnp.where(wide > 0, 1.0, 0.0) / jnp.maximum(wide, 1.0)
    for name in ("u0", "v2", "bias", "v1", "u1"):
        loads[name].wait()

    for r in range(LAYERS):
        last = r == LAYERS - 1
        start2(r, 0)
        start2(r, 1)
        if r == 0:
            share_w()
        start3(r, 0)
        start3(r, 1)
        if r == 1:
            settle(wrecv.at[0 : SIDE - 1], wr_sem)
            for c in range(SIDE):
                wturn[c] = wrecv[c].T
        if last:
            cot = grads[0]
            pre[...] = scale[...] * (
                grads[1] * ups[1] + grads[2] * ups[0] + grads[2] + cot * bias_ref[2:3, :]
            )
            cots[...] = scale[...] * cot
        up = dot(finish(r, 0), u_ref[r])
        if last:
            pre[...] = pre[...] + cots[...] * up
        else:
            up = up + bias_ref[r : r + 1, :]
            ups[r] = up
            state[...] = base[...].astype(F32) * up + state[...]
            start_forward(r + 1)
        down = dot(finish(r, 1), v_ref[LAYERS - 1 - r], NT)
        if not last:
            grads[r + 1] = grads[r] + down
            start_backward(r + 1)

    scaled = pre[...] + scale[...] * down
    parts = [scaled[:, j * E : (j + 1) * E] for j in range(FEATS)]
    parts = [part.astype(BF16) for part in parts]
    for c in range(SIDE):
        block = jnp.zeros((SAMPLES, E), BF16)
        for j in range(FEATS):
            block = block + inside(c, j).astype(BF16) * parts[j]
        dsend[c] = block
    for d in XORDER:
        to = lax.rem(x + d, SIDE)
        copy(
            dsend.at[to], drecv.at[group], ds_sem, dr_sem.at[d], (node, to * CORES + core)
        ).start()
    copy(dsend.at[x], drecv.at[group], fs_sem, fr_sem.at[0], sibling).start()
    drecv[group] = dsend[x]

    for r in range(LAYERS):
        for k in range(2):
            settle(recv1.at[r, k], s1_sem.at[r, k])
            settle(recv1.at[r, k], s2_sem.at[r, k])
            settle(recv1.at[r, k], s3_sem.at[r, k])
    settle(wrecv.at[0 : SIDE - 1], ws_sem)

    mine = proj_ref[pl.ds(pl.multiple_of(group * PIECE, PIECE), PIECE), :]
    half = pl.ds(pl.multiple_of(core * PIECE, PIECE), PIECE)
    other = pl.ds(pl.multiple_of((1 - core) * PIECE, PIECE), PIECE)

    def use(d):
        chip = lax.rem(x + SIDE - d, SIDE)
        settle(drecv.at[chip * CORES + 1 - core], fr_sem.at[d])
        pair = drecv[pl.ds(chip * CORES, CORES)].reshape(CORES * SAMPLES, E)
        at = pl.ds(pl.multiple_of(chip * (CORES * SAMPLES), CORES * SAMPLES), CORES * SAMPLES)
        row_ref[:, at] = dot(mine, pair, NT).astype(BF16)

    pgown[...] = dot(wturn[x], dsend[x])
    waiting = [0]
    for d in XORDER:
        chip = lax.rem(x + SIDE - d, SIDE)
        block = drecv.at[chip * CORES + core]
        settle(block, dr_sem.at[d])
        copy(block, block, fs_sem, fr_sem.at[d], sibling).start()
        pgown[...] = pgown[...] + dot(wturn[chip], block[...])
        waiting.append(d)
        if d == XORDER[-1]:
            parting = copy(pgown.at[other], pgin, ps_sem, pr_sem, sibling)
            parting.start()
        if len(waiting) > 5:
            use(waiting.pop(0))
    for d in waiting:
        use(d)
    parting.wait()
    pg_ref[...] = pgown[half, :] + pgin[...]
    settle(drecv.at[0 : SIDE - 1], ds_sem)
    settle(drecv.at[0:SIDE], fs_sem)


def store_kernel(row_ref, pg_ref, row_out, pg_out, sems):
    moves = [
        pltpu.make_async_copy(row_ref, row_out, sems.at[0]),
        pltpu.make_async_copy(pg_ref, pg_out, sems.at[1]),
    ]
    for move in moves:
        move.start()
    for move in moves:
        move.wait()


def store(row_grads, proj_grad):
    here = pl.BlockSpec(memory_space=pl.ANY)
    return pl.pallas_call(
        store_kernel,
        out_shape=(
            pltpu.HBM(row_grads.shape, row_grads.dtype),
            pltpu.HBM(proj_grad.shape, proj_grad.dtype),
        ),
        in_specs=[here, here],
        out_specs=(here, here),
        scratch_shapes=[pltpu.SemaphoreType.DMA((2,))],
        compiler_params=pltpu.CompilerParams(vmem_limit_bytes=4 * 1024 * 1024),
    )(*[pltpu.with_memory_space_constraint(a, pltpu.VMEM) for a in (row_grads, proj_grad)])


def on_device(pooled, counts, dims, proj, v_weight, u_weight, bias, cotangent):
    vmem = pl.BlockSpec(memory_space=pltpu.VMEM)
    hbm = pl.BlockSpec(memory_space=pl.ANY)
    dma = pltpu.SemaphoreType.DMA
    pair = (LAYERS, 2)
    inputs = (dims, counts.T, pooled, proj, v_weight, u_weight, bias, cotangent)
    results = pl.pallas_call(
        kernel,
        out_shape=(
            jax.ShapeDtypeStruct((PIECE, GROUPS * SAMPLES), BF16),
            jax.ShapeDtypeStruct((PIECE, E), F32),
        ),
        in_specs=[hbm] * 8,
        out_specs=(vmem, vmem),
        scratch_shapes=[pltpu.SMEM(dims.shape, dims.dtype)]
        + [pltpu.VMEM(a.shape, a.dtype) for a in inputs[1:]]
        + [
            pltpu.VMEM((SAMPLES, WIDTH), BF16),
            pltpu.VMEM((SAMPLES, WIDTH), F32),
            pltpu.VMEM((LAYERS, SAMPLES, WIDTH), F32),
            pltpu.VMEM((LAYERS - 1, SAMPLES, WIDTH), F32),
            pltpu.VMEM((SAMPLES, WIDTH), F32),
            pltpu.VMEM((SAMPLES, WIDTH), F32),
            pltpu.VMEM((SAMPLES, WIDTH), F32),
            pltpu.VMEM(pair + (SIDE, SHARD, E), BF16),
            pltpu.VMEM(pair + (SIDE - 1, SHARD, E), BF16),
            pltpu.VMEM(pair + (SHARD, E), BF16),
            pltpu.VMEM(pair + (SIDE - 1, SHARD, E), BF16),
            pltpu.VMEM(pair + (SIDE, SHARD, E), BF16),
            pltpu.VMEM((SIDE, SAMPLES, E), BF16),
            pltpu.VMEM((SIDE, SAMPLES, E), BF16),
            pltpu.VMEM((SIDE, E, SAMPLES), BF16),
            pltpu.VMEM((SIDE, SAMPLES, E), BF16),
            pltpu.VMEM((GROUPS, SAMPLES, E), BF16),
            pltpu.VMEM((E, E), F32),
            pltpu.VMEM((PIECE, E), F32),
            dma((12,)),
            dma(pair), dma(pair), dma(pair), dma(pair), dma(pair), dma(pair),
            dma, dma, dma, dma((SIDE,)), dma, dma((SIDE,)), dma, dma,
        ],
        compiler_params=pltpu.CompilerParams(
            collective_id=0, has_side_effects=True, vmem_limit_bytes=32 * 1024 * 1024
        ),
        cost_estimate=pl.CostEstimate(
            flops=1_500_000_000, bytes_accessed=3_000_000, transcendentals=0
        ),
    )(*[pltpu.with_memory_space_constraint(a, pltpu.HBM) for a in inputs])
    return store(*results)


def solution(mesh):
    in_specs = (
        P("xnode", "node"),
        P("xnode", "node"),
        P("node"),
        P("node", None),
        P(None, "node", None),
        P(None, None, "node"),
        P(None, "node"),
        P("xnode", "node"),
    )
    out_specs = (P(("node", "xnode"), None), P(("node", "xnode"), None))
    return jax.shard_map(
        on_device, mesh=mesh, in_specs=in_specs, out_specs=out_specs, check_vma=False
    )
```
